768 devices in a mesh: seq: 16 (over x, y_hi, core), head: 12 (over z), rep: 4 (over y_lo).
Axes of the slice: x: 4, y: 8 (y_hi: 2, y_lo: 4; y = y_hi * 4 + y_lo), z: 12, core: 2. Of those that a mesh axis runs over, the one named last changes fastest.
Arguments:
- queries: bfloat16 [64, 1536, 3072], P(('seq', 'rep'), 'head'), may hold values from -18 to 18, as said below
- keys: bfloat16 [64, 1536, 3072], P(('seq', 'rep'), 'head'), may hold values from -18 to 18, as said below
- values: bfloat16 [64, 1536, 3072], P(('seq', 'rep'), 'head'), may hold values from -6 to 6
- text_kv: bfloat16 [64, 384, 6144], P(('seq', 'rep'), 'head'), may hold values from -18 to 18, as said below
- cotangent: bfloat16 [64, 1536, 3072], P(('seq', 'rep'), None, 'head'), may hold values from -6 to 6
Outputs:
- attended: bfloat16 [64, 1536, 3072], P(('seq', 'rep'), None, 'head')
- text_grad: bfloat16 [64, 384, 6144], P(('seq', 'rep'), 'head')
The draws below stay inside these ranges and needn't reach their ends.
Inputs may be any that keep to these rules, and one draw needn't show every extreme that they name: `queries`: normal-like entries of order one. `keys`: normal-like entries of order one. `text_kv`: normal-like entries of order one.
All inputs are finite; a program needn't handle non-finite values.
Results may differ from the reference program's by a relative error of at most 0.007.
Values may be sent and summed in bfloat16 or wider, within the bound.
A program may use at most 32 MiB of HBM per device.

```python
import jax
import jax.numpy as jnp
from jax import lax

HEADS = 24
HD = 128
TXT = 384
L = 1536
CLIPS = 64


def draw_queries(key, part):
    drawn = jax.random.truncated_normal(jax.random.fold_in(key, 1), -4.0, 4.0, (CLIPS, L, HEADS * HD), jnp.float32)
    return drawn.astype(jnp.bfloat16)


def draw_keys(key, part):
    drawn = jax.random.truncated_normal(jax.random.fold_in(key, 2), -4.0, 4.0, (CLIPS, L, HEADS * HD), jnp.float32)
    return drawn.astype(jnp.bfloat16)


def draw_text_kv(key, part):
    drawn = jax.random.truncated_normal(jax.random.fold_in(key, 3), -4.0, 4.0, (CLIPS, TXT, HEADS, 2, HD), jnp.float32)
    return drawn.reshape(CLIPS, TXT, HEADS * 2 * HD).astype(jnp.bfloat16)


def level_of(stream_key, extent, shards, smallest, high):
    loudness = 1.0
    for axis_at, blocks in shards:
        draws = jax.random.uniform(jax.random.fold_in(jax.random.fold_in(stream_key, 6), axis_at), (blocks,), jnp.float32, smallest / len(shards), high / len(shards))
        loudness = loudness * jnp.repeat(jnp.exp(draws), extent[axis_at] // blocks).reshape((-1,) + (1,) * (len(extent) - 1 - axis_at))
    return loudness


def noise(key, extent, spread, most, cuts=(), kind=jnp.bfloat16):
    gain = level_of(key, extent, cuts, -0.22, 0.18) if cuts else 1.0
    result = jax.random.normal(key, extent, jnp.float32) * spread * gain
    return jnp.minimum(jnp.maximum(result, -most), most).astype(kind)


def setup_inputs(seed: int = 0) -> dict:
    key_list = jax.random.split(jax.random.key(seed), 6)
    queries = draw_queries(jax.random.fold_in(key_list[5], 71), 0)
    keys = draw_keys(jax.random.fold_in(key_list[5], 71), 0)
    values = noise(key_list[2], (CLIPS, L, HEADS * HD), 1.0, 6.0, ((0, 64), (1, 12)))
    text_kv = draw_text_kv(jax.random.fold_in(key_list[5], 71), 0)
    cotangent = noise(key_list[4], (CLIPS, L, HEADS * HD), 1.0, 6.0, ((0, 64), (2, 12)))
    return {"queries": queries, "keys": keys, "values": values, "text_kv": text_kv, "cotangent": cotangent}


def softmax_rows(scores):
    top = jnp.max(scores, axis=-1, keepdims=True)
    weights = jnp.exp(scores - top)
    return weights / jnp.sum(weights, axis=-1, keepdims=True)


def block_rows(total):
    return 512 if total % 512 == 0 else total


def attend_block(query_block, grad_block, key_all, value_all, text_keys, text_values, scale):
    query_f = query_block.astype(jnp.float32)
    grad_f = grad_block.astype(jnp.float32)
    scores = jnp.einsum("bgd,lgd->gbl", query_f, key_all.astype(jnp.float32)) * scale
    probs = softmax_rows(scores).astype(jnp.bfloat16)
    self_out = jnp.einsum("gbl,lgd->bgd", probs.astype(jnp.float32), value_all.astype(jnp.float32))
    text_keys_f = text_keys.astype(jnp.float32)
    text_values_f = text_values.astype(jnp.float32)
    cross_scores = jnp.einsum("bgd,tgd->gbt", query_f, text_keys_f) * scale
    cross_probs = softmax_rows(cross_scores)
    cross_rounded = cross_probs.astype(jnp.bfloat16).astype(jnp.float32)
    cross_out = jnp.einsum("gbt,tgd->bgd", cross_rounded, text_values_f)
    attended = (self_out + cross_out).astype(jnp.bfloat16)
    grad_values = jnp.einsum("gbt,bgd->tgd", cross_rounded, grad_f)
    dprobs = jnp.einsum("bgd,tgd->gbt", grad_f, text_values_f)
    dscores = cross_probs * (dprobs - jnp.sum(dprobs * cross_probs, axis=-1, keepdims=True))
    dscores = dscores.astype(jnp.bfloat16).astype(jnp.float32)
    grad_keys = jnp.einsum("gbt,bgd->tgd", dscores, query_f) * scale
    return attended, grad_keys, grad_values


def reference(queries, keys, values, text_kv, cotangent):
    scale = float(HD) ** -0.5
    block = block_rows(L)
    count_blocks = L // block

    def one_clip(carry, inputs):
        query_clip, key_clip, value_clip, text_clip, grad_clip = inputs
        text_heads = text_clip.reshape(TXT, HEADS, 2, HD)
        text_keys = text_heads[:, :, 0, :]
        text_values = text_heads[:, :, 1, :]
        query_heads = query_clip.reshape(count_blocks, block, HEADS, HD)
        grad_heads = grad_clip.reshape(count_blocks, block, HEADS, HD)
        key_heads = key_clip.reshape(L, HEADS, HD)
        value_heads = value_clip.reshape(L, HEADS, HD)

        def one_block(inner, pieces):
            attended, grad_keys, grad_values = attend_block(pieces[0], pieces[1], key_heads, value_heads, text_keys, text_values, scale)
            return (inner[0] + grad_keys, inner[1] + grad_values), attended

        zeros = jnp.zeros((TXT, HEADS, HD), jnp.float32)
        (grad_keys, grad_values), outputs = lax.scan(one_block, (zeros, zeros), (query_heads, grad_heads))
        grads = jnp.stack([grad_keys, grad_values], axis=2).reshape(TXT, HEADS * 2 * HD).astype(jnp.bfloat16)
        return carry, (outputs.reshape(L, HEADS * HD), grads)

    _, (attended, text_grad) = lax.scan(one_clip, jnp.zeros((), jnp.float32), (queries, keys, values, text_kv, cotangent))
    return attended, text_grad
```

```python
import functools
import math

import jax
import jax.numpy as jnp
from jax import lax
from jax.experimental import pallas as pl
from jax.experimental.pallas import tpu as pltpu
from jax.sharding import PartitionSpec as P

HD = 128
MESH = pl.DeviceIdType.MESH
BF16 = jnp.bfloat16
F32 = jnp.float32


def dot(a, b, ca, cb):
    return lax.dot_general(a, b, (((ca,), (cb,)), ((), ())), preferred_element_type=F32)


def near_first(n):
    order = []
    for d in range(1, n // 2 + 1):
        order.append(d)
        if n - d != d:
            order.append(n - d)
    return order


def kernel(
    n, q_in, k_in, v_in, t_in, g_in, att_out, tg_out,
    q_buf, k_buf, v_buf, t_buf, g_buf, p_buf, cross_buf, att_buf, dk_acc, dv_acc, tg_buf,
    send_sem, recv_sem, local_sem, out_sem, gsend_sem, grecv_sem,
):
    me = lax.axis_index("head")
    rows = q_in.shape[0]
    trows = t_in.shape[0]
    width = q_buf.shape[1]
    twidth = t_buf.shape[1]
    length = q_buf.shape[0]
    groups = width // HD
    factor = HD ** -0.5 * math.log2(math.e)

    own = []
    for a, (src, dst, h, w) in enumerate(
        ((t_in, t_buf, trows, twidth), (q_in, q_buf, rows, width), (k_in, k_buf, rows, width), (v_in, v_buf, rows, width))
    ):
        copy = pltpu.make_async_copy(
            src.at[:, pl.ds(pl.multiple_of(me * w, w), w)],
            dst.at[pl.ds(pl.multiple_of(me * h, h), h), :],
            local_sem.at[a],
        )
        copy.start()
        own.append(copy)
    g_copy = pltpu.make_async_copy(g_in, g_buf, local_sem.at[4])
    g_copy.start()

    barrier = pltpu.get_barrier_semaphore()
    for d in range(1, n):
        pl.semaphore_signal(barrier, inc=1, device_id={"head": lax.rem(me + d, n)}, device_id_type=MESH)
    pl.semaphore_wait(barrier, n - 1)

    sends = [[], [], [], []]
    for a, (src, dst, h, w) in enumerate(
        ((t_in, t_buf, trows, twidth), (q_in, q_buf, rows, width), (k_in, k_buf, rows, width), (v_in, v_buf, rows, width))
    ):
        for d in near_first(n):
            to = lax.rem(me + d, n)
            copy = pltpu.make_async_remote_copy(
                src_ref=src.at[:, pl.ds(pl.multiple_of(to * w, w), w)],
                dst_ref=dst.at[pl.ds(pl.multiple_of(me * h, h), h), :],
                send_sem=send_sem.at[a, d],
                recv_sem=recv_sem.at[a, d],
                device_id={"head": to},
                device_id_type=MESH,
            )
            copy.start()
            sends[a].append(copy)

    def arrive(a):
        own[a].wait()
        for copy in sends[a]:
            copy.wait_recv()

    g_copy.wait()
    arrive(0)
    arrive(1)

    dk_acc[...] = jnp.zeros_like(dk_acc)
    dv_acc[...] = jnp.zeros_like(dv_acc)
    cross_rows = 256

    def cross_step(i, carry):
        at = pl.ds(pl.multiple_of(i * cross_rows, cross_rows), cross_rows)
        for h in range(groups):
            cols = pl.ds(h * HD, HD)
            q = q_buf[at, cols]
            g = g_buf[at, cols]
            kt = t_buf[:, pl.ds(2 * h * HD, HD)]
            vt = t_buf[:, pl.ds((2 * h + 1) * HD, HD)]
            x = dot(kt, q, 1, 1)
            e = jnp.exp2((x - jnp.max(x, axis=0, keepdims=True)) * factor)
            r = e * (1.0 / jnp.sum(e, axis=0, keepdims=True))
            rb = r.astype(BF16)
            dr = dot(vt, g, 1, 1)
            dx = (r * (dr - jnp.sum(dr * r, axis=0, keepdims=True))).astype(BF16)
            dk_acc[h] += dot(dx, q, 1, 0)
            dv_acc[h] += dot(rb, g, 1, 0)
            cross_buf[at, cols] = dot(rb, vt, 0, 0)
        return carry

    lax.fori_loop(0, length // cross_rows, cross_step, 0)
    for h in range(groups):
        tg_buf[:, pl.ds(2 * h * HD, HD)] = (dk_acc[h] * (HD ** -0.5)).astype(BF16)
        tg_buf[:, pl.ds((2 * h + 1) * HD, HD)] = dv_acc[h].astype(BF16)
    own_grad = pltpu.make_async_copy(
        tg_buf.at[pl.ds(pl.multiple_of(me * trows, trows), trows), :],
        tg_out.at[:, pl.ds(pl.multiple_of(me * twidth, twidth), twidth)],
        local_sem.at[5],
    )
    own_grad.start()
    returns = []
    for d in near_first(n):
        to = lax.rem(me + d, n)
        copy = pltpu.make_async_remote_copy(
            src_ref=tg_buf.at[pl.ds(pl.multiple_of(to * trows, trows), trows), :],
            dst_ref=tg_out.at[:, pl.ds(pl.multiple_of(me * twidth, twidth), twidth)],
            send_sem=gsend_sem.at[d],
            recv_sem=grecv_sem.at[d],
            device_id={"head": to},
            device_id_type=MESH,
        )
        copy.start()
        returns.append(copy)

    arrive(2)
    block = 256

    def score_step(i, carry):
        at = pl.ds(pl.multiple_of(i * block, block), block)
        for h in range(groups):
            cols = pl.ds(h * HD, HD)
            s = dot(q_buf[at, cols], k_buf[:, cols], 1, 1)
            top = jnp.max(s, axis=1, keepdims=True)
            p_buf[h, at, :] = jnp.exp2((s - top) * factor).astype(BF16)
        return carry

    lax.fori_loop(0, length // block, score_step, 0)

    arrive(3)

    def out_copy(i):
        at = pl.ds(pl.multiple_of(i * block, block), block)
        return pltpu.make_async_copy(att_buf.at[at, :], att_out.at[at, :], out_sem.at[i])

    def value_step(i, carry):
        at = pl.ds(pl.multiple_of(i * block, block), block)
        for h in range(groups):
            cols = pl.ds(h * HD, HD)
            v = v_buf[:, cols]
            both = dot(p_buf[h, at, :], jnp.concatenate([v, jnp.ones_like(v)], axis=1), 1, 0)
            att_buf[at, cols] = (both[:, :HD] / both[:, HD:] + cross_buf[at, cols]).astype(BF16)
        out_copy(i).start()
        return carry

    lax.fori_loop(0, length // block, value_step, 0)

    for a in range(4):
        for copy in sends[a]:
            copy.wait_send()
    own_grad.wait()
    for copy in returns:
        copy.wait()
    for i in range(length // block):
        out_copy(i).wait()


def per_device(n, queries, keys, values, text_kv, cotangent):
    rows, columns = queries.shape[1:]
    trows, tcolumns = text_kv.shape[1:]
    length, width = cotangent.shape[1:]
    twidth = tcolumns // n
    text = trows * n
    groups = width // HD
    attended, grad = pl.pallas_call(
        functools.partial(kernel, n),
        out_shape=(
            jax.ShapeDtypeStruct((length, width), BF16),
            jax.ShapeDtypeStruct((trows, tcolumns), BF16),
        ),
        in_specs=[pl.BlockSpec(memory_space=pl.ANY)] * 5,
        out_specs=(pl.BlockSpec(memory_space=pl.ANY),) * 2,
        scratch_shapes=[
            pltpu.VMEM((length, width), BF16),
            pltpu.VMEM((length, width), BF16),
            pltpu.VMEM((length, width), BF16),
            pltpu.VMEM((text, twidth), BF16),
            pltpu.VMEM((length, width), BF16),
            pltpu.VMEM((groups, length, length), BF16),
            pltpu.VMEM((length, width), F32),
            pltpu.VMEM((length, width), BF16),
            pltpu.VMEM((groups, text, HD), F32),
            pltpu.VMEM((groups, text, HD), F32),
            pltpu.VMEM((text, twidth), BF16),
            pltpu.SemaphoreType.DMA((4, n)),
            pltpu.SemaphoreType.DMA((4, n)),
            pltpu.SemaphoreType.DMA((6,)),
            pltpu.SemaphoreType.DMA((length // 256,)),
            pltpu.SemaphoreType.DMA((n,)),
            pltpu.SemaphoreType.DMA((n,)),
        ],
        compiler_params=pltpu.CompilerParams(
            collective_id=0, has_side_effects=True, vmem_limit_bytes=60 * 2**20
        ),
    )(queries[0], keys[0], values[0], text_kv[0], cotangent[0])
    return attended[None], grad[None]


def solution(mesh):
    split = P(("seq", "rep"), "head", None)
    kept = P(("seq", "rep"), None, "head")
    return jax.shard_map(
        functools.partial(per_device, mesh.shape["head"]),
        mesh=mesh,
        in_specs=(split, split, split, split, kept),
        out_specs=(kept, split),
        check_vma=False,
    )
```

```python
import functools
import math

import jax
import jax.numpy as jnp
from jax import lax
from jax.experimental import pallas as pl
from jax.experimental.pallas import tpu as pltpu
from jax.sharding import PartitionSpec as P

HD = 128
MESH = pl.DeviceIdType.MESH
BF16 = jnp.bfloat16
F32 = jnp.float32


def dot(a, b, ca, cb):
    return lax.dot_general(a, b, (((ca,), (cb,)), ((), ())), preferred_element_type=F32)


def near_first(n, at):
    order = []
    for d in range(1, n // 2 + 1):
        order.append((at + d) % n)
        if n - d != d:
            order.append((at - d) % n)
    return order


def below_first(n, at):
    return [to for to in near_first(n, at) if to < at] + list(range(at + 1, n))


def pick(me, column):
    value = jnp.int32(column[0])
    for at in range(1, len(column)):
        value = jnp.where(me == at, jnp.int32(column[at]), value)
    return value


def peers(n, me, order):
    table = [order(n, at) for at in range(n)]
    return [pick(me, [row[j] for row in table]) for j in range(n - 1)]


def kernel(
    n, q_in, k_in, v_in, t_in, g_in, att_out, tg_out,
    q_buf, k_buf, v_buf, t_buf, g_buf, p_buf, cross_buf, att_buf, dk_acc, dv_acc, tg_buf,
    send_sem, recv_sem, local_sem, out_sem, gsend_sem, grecv_sem, in_sem,
):
    me = lax.axis_index("head")
    rows = q_in.shape[0]
    trows = t_in.shape[0]
    width = q_buf.shape[1]
    twidth = t_buf.shape[1]
    length = q_buf.shape[0]
    groups = width // HD
    factor = HD ** -0.5 * math.log2(math.e)

    own = []
    for a, (src, dst, h, w) in enumerate(
        ((t_in, t_buf, trows, twidth), (q_in, q_buf, rows, width), (k_in, k_buf, rows, width), (v_in, v_buf, rows, width))
    ):
        copy = pltpu.make_async_copy(
            src.at[:, pl.ds(pl.multiple_of(me * w, w), w)],
            dst.at[pl.ds(pl.multiple_of(me * h, h), h), :],
            local_sem.at[a],
        )
        copy.start()
        own.append(copy)
    g_copy = pltpu.make_async_copy(g_in, g_buf, local_sem.at[4])
    g_copy.start()

    barrier = pltpu.get_barrier_semaphore()

    @pl.when(me > 0)
    def _():
        pl.semaphore_wait(barrier, 1)

    @pl.when(me < n - 1)
    def _():
        pl.semaphore_signal(barrier, inc=1, device_id={"head": lax.rem(me + 1, n)}, device_id_type=MESH)

    for w in range(n - 1):

        @pl.when(w < me)
        def _(w=w):
            pl.semaphore_signal(in_sem.at[me], inc=1, device_id={"head": w}, device_id_type=MESH)

    arrays = ((t_in, t_buf, trows, twidth), (q_in, q_buf, rows, width), (k_in, k_buf, rows, width), (v_in, v_buf, rows, width))

    def block_copy(a, source, to, sem):
        src, dst, h, w = arrays[a]
        return pltpu.make_async_remote_copy(
            src_ref=src.at[:, pl.ds(pl.multiple_of(to * w, w), w)],
            dst_ref=dst.at[pl.ds(pl.multiple_of(source * h, h), h), :],
            send_sem=send_sem.at[a, sem],
            recv_sem=recv_sem.at[a, source],
            device_id={"head": to},
            device_id_type=MESH,
        )

    for to in peers(n, me, below_first):

        @pl.when(to > me)
        def _():
            pl.semaphore_wait(in_sem.at[to], 1)

        block_copy(0, me, to, to).start()
        block_copy(1, me, to, to).start()

    for a in (2, 3):
        for to in peers(n, me, near_first):
            block_copy(a, me, to, to).start()

    others = [lax.rem(me + d, n) for d in range(1, n)]

    def arrive(a):
        own[a].wait()
        for other in others:
            block_copy(a, other, other, other).wait_recv()

    g_copy.wait()
    arrive(0)
    arrive(1)

    dk_acc[...] = jnp.zeros_like(dk_acc)
    dv_acc[...] = jnp.zeros_like(dv_acc)
    cross_rows = 256

    def cross_step(i, carry):
        at = pl.ds(pl.multiple_of(i * cross_rows, cross_rows), cross_rows)
        for h in range(groups):
            cols = pl.ds(h * HD, HD)
            q = q_buf[at, cols]
            g = g_buf[at, cols]
            kt = t_buf[:, pl.ds(2 * h * HD, HD)]
            vt = t_buf[:, pl.ds((2 * h + 1) * HD, HD)]
            x = dot(kt, q, 1, 1)
            e = jnp.exp2((x - jnp.max(x, axis=0, keepdims=True)) * factor)
            r = e * (1.0 / jnp.sum(e, axis=0, keepdims=True))
            rb = r.astype(BF16)
            dr = dot(vt, g, 1, 1)
            dx = (r * (dr - jnp.sum(dr * r, axis=0, keepdims=True))).astype(BF16)
            dk_acc[h] += dot(dx, q, 1, 0)
            dv_acc[h] += dot(rb, g, 1, 0)
            cross_buf[at, cols] = dot(rb, vt, 0, 0)
        return carry

    lax.fori_loop(0, length // cross_rows, cross_step, 0)
    for h in range(groups):
        tg_buf[:, pl.ds(2 * h * HD, HD)] = (dk_acc[h] * (HD ** -0.5)).astype(BF16)
        tg_buf[:, pl.ds((2 * h + 1) * HD, HD)] = dv_acc[h].astype(BF16)
    own_grad = pltpu.make_async_copy(
        tg_buf.at[pl.ds(pl.multiple_of(me * trows, trows), trows), :],
        tg_out.at[:, pl.ds(pl.multiple_of(me * twidth, twidth), twidth)],
        local_sem.at[5],
    )
    own_grad.start()
    def grad_copy(source, to, sem):
        return pltpu.make_async_remote_copy(
            src_ref=tg_buf.at[pl.ds(pl.multiple_of(to * trows, trows), trows), :],
            dst_ref=tg_out.at[:, pl.ds(pl.multiple_of(source * twidth, twidth), twidth)],
            send_sem=gsend_sem.at[sem],
            recv_sem=grecv_sem.at[source],
            device_id={"head": to},
            device_id_type=MESH,
        )

    for to in peers(n, me, near_first):
        grad_copy(me, to, to).start()

    arrive(2)
    block = 256

    def score_step(i, carry):
        at = pl.ds(pl.multiple_of(i * block, block), block)
        for h in range(groups):
            cols = pl.ds(h * HD, HD)
            s = dot(q_buf[at, cols], k_buf[:, cols], 1, 1)
            top = jnp.max(s, axis=1, keepdims=True)
            p_buf[h, at, :] = jnp.exp2((s - top) * factor).astype(BF16)
        return carry

    lax.fori_loop(0, length // block, score_step, 0)

    arrive(3)

    def out_copy(i):
        at = pl.ds(pl.multiple_of(i * block, block), block)
        return pltpu.make_async_copy(att_buf.at[at, :], att_out.at[at, :], out_sem.at[i])

    def value_step(i, carry):
        at = pl.ds(pl.multiple_of(i * block, block), block)
        for h in range(groups):
            cols = pl.ds(h * HD, HD)
            v = v_buf[:, cols]
            both = dot(p_buf[h, at, :], jnp.concatenate([v, jnp.ones_like(v)], axis=1), 1, 0)
            att_buf[at, cols] = (both[:, :HD] / both[:, HD:] + cross_buf[at, cols]).astype(BF16)
        out_copy(i).start()
        return carry

    lax.fori_loop(0, length // block, value_step, 0)

    own_grad.wait()
    for other in others:
        for a in range(4):
            block_copy(a, me, other, other).wait_send()
        grad_copy(me, other, other).wait_send()
        grad_copy(other, other, other).wait_recv()
    for i in range(length // block):
        out_copy(i).wait()


def place(a_in, b_in, a_out, b_out, sems):
    copies = [
        pltpu.make_async_copy(a_in, a_out, sems.at[0]),
        pltpu.make_async_copy(b_in, b_out, sems.at[1]),
    ]
    for copy in copies:
        copy.start()
    for copy in copies:
        copy.wait()


def per_device(n, queries, keys, values, text_kv, cotangent):
    rows, columns = queries.shape[1:]
    trows, tcolumns = text_kv.shape[1:]
    length, width = cotangent.shape[1:]
    twidth = tcolumns // n
    text = trows * n
    groups = width // HD
    attended, grad = pl.pallas_call(
        functools.partial(kernel, n),
        out_shape=(
            pltpu.VMEM((length, width), BF16),
            pltpu.VMEM((trows, tcolumns), BF16),
        ),
        in_specs=[pl.BlockSpec(memory_space=pl.ANY)] * 5,
        out_specs=(pl.BlockSpec(memory_space=pl.ANY),) * 2,
        scratch_shapes=[
            pltpu.VMEM((length, width), BF16),
            pltpu.VMEM((length, width), BF16),
            pltpu.VMEM((length, width), BF16),
            pltpu.VMEM((text, twidth), BF16),
            pltpu.VMEM((length, width), BF16),
            pltpu.VMEM((groups, length, length), BF16),
            pltpu.VMEM((length, width), F32),
            pltpu.VMEM((length, width), BF16),
            pltpu.VMEM((groups, text, HD), F32),
            pltpu.VMEM((groups, text, HD), F32),
            pltpu.VMEM((text, twidth), BF16),
            pltpu.SemaphoreType.DMA((4, n)),
            pltpu.SemaphoreType.DMA((4, n)),
            pltpu.SemaphoreType.DMA((6,)),
            pltpu.SemaphoreType.DMA((length // 256,)),
            pltpu.SemaphoreType.DMA((n,)),
            pltpu.SemaphoreType.DMA((n,)),
            pltpu.SemaphoreType.REGULAR((n,)),
        ],
        compiler_params=pltpu.CompilerParams(
            collective_id=0, has_side_effects=True, vmem_limit_bytes=40 * 2**20
        ),
    )(*(pltpu.with_memory_space_constraint(x[0], pltpu.HBM) for x in (queries, keys, values, text_kv, cotangent)))
    attended, grad = pl.pallas_call(
        place,
        out_shape=(
            jax.ShapeDtypeStruct((length, width), BF16),
            jax.ShapeDtypeStruct((trows, tcolumns), BF16),
        ),
        in_specs=[pl.BlockSpec(memory_space=pl.ANY)] * 2,
        out_specs=(pl.BlockSpec(memory_space=pltpu.HBM),) * 2,
        scratch_shapes=[pltpu.SemaphoreType.DMA((2,))],
    )(*(pltpu.with_memory_space_constraint(x, pltpu.VMEM) for x in (attended, grad)))
    return attended[None], grad[None]


def solution(mesh):
    split = P(("seq", "rep"), "head", None)
    kept = P(("seq", "rep"), None, "head")
    return jax.shard_map(
        functools.partial(per_device, mesh.shape["head"]),
        mesh=mesh,
        in_specs=(split, split, split, split, kept),
        out_specs=(kept, split),
        check_vma=False,
    )
```

```python
import functools
import math

import jax
import jax.numpy as jnp
from jax import lax
from jax.experimental import pallas as pl
from jax.experimental.pallas import tpu as pltpu
from jax.sharding import PartitionSpec as P

HD = 128
MESH = pl.DeviceIdType.MESH
BF16 = jnp.bfloat16
F32 = jnp.float32


def dot(a, b, ca, cb):
    return lax.dot_general(a, b, (((ca,), (cb,)), ((), ())), preferred_element_type=F32)


def near_first(n, at):
    order = []
    for d in range(1, n // 2 + 1):
        order.append((at + d) % n)
        if n - d != d:
            order.append((at - d) % n)
    return order


def below_first(n, at):
    return [to for to in near_first(n, at) if to < at] + list(range(at + 1, n))


def ascending(n, at):
    return [to for to in range(n) if to != at]


def pick(me, column):
    value = jnp.int32(column[0])
    for at in range(1, len(column)):
        value = jnp.where(me == at, jnp.int32(column[at]), value)
    return value


def peers(n, me, order):
    table = [order(n, at) for at in range(n)]
    return [pick(me, [row[j] for row in table]) for j in range(n - 1)]


def kernel(
    n, q_in, k_in, v_in, t_in, g_in, att_out, tg_out,
    q_buf, k_buf, v_buf, t_buf, g_buf, p_buf, cross_buf, att_buf, dk_acc, dv_acc, tg_buf, relay_buf,
    send_sem, recv_sem, local_sem, out_sem, gsend_sem, grecv_sem, in_sem, relay_sem, pass_sem,
):
    me = lax.axis_index("head")
    rows = q_in.shape[0]
    trows = t_in.shape[0]
    width = q_buf.shape[1]
    twidth = t_buf.shape[1]
    length = q_buf.shape[0]
    groups = width // HD
    factor = HD ** -0.5 * math.log2(math.e)

    barrier = pltpu.get_barrier_semaphore()

    @pl.when(me > 0)
    def _():
        pl.semaphore_wait(barrier, 1)

    @pl.when(me < n - 1)
    def _():
        pl.semaphore_signal(barrier, inc=1, device_id={"head": lax.rem(me + 1, n)}, device_id_type=MESH)

    for w in range(n - 1):

        @pl.when(w < me)
        def _(w=w):
            pl.semaphore_signal(in_sem.at[me], inc=1, device_id={"head": w}, device_id_type=MESH)

    own = []
    for a, (src, dst, h, w) in enumerate(
        ((t_in, t_buf, trows, twidth), (q_in, q_buf, rows, width), (k_in, k_buf, rows, width), (v_in, v_buf, rows, width))
    ):
        copy = pltpu.make_async_copy(
            src.at[:, pl.ds(pl.multiple_of(me * w, w), w)],
            dst.at[pl.ds(pl.multiple_of(me * h, h), h), :],
            local_sem.at[a],
        )
        copy.start()
        own.append(copy)
    g_copy = pltpu.make_async_copy(g_in, g_buf, local_sem.at[4])
    g_copy.start()

    arrays = ((t_in, t_buf, trows, twidth), (q_in, q_buf, rows, width), (k_in, k_buf, rows, width), (v_in, v_buf, rows, width))

    def block_copy(a, source, to, sem):
        src, dst, h, w = arrays[a]
        return pltpu.make_async_remote_copy(
            src_ref=src.at[:, pl.ds(pl.multiple_of(to * w, w), w)],
            dst_ref=dst.at[pl.ds(pl.multiple_of(source * h, h), h), :],
            send_sem=send_sem.at[a, sem],
            recv_sem=recv_sem.at[a, source],
            device_id={"head": to},
            device_id_type=MESH,
        )

    for to in peers(n, me, below_first):

        @pl.when(to > me)
        def _():
            pl.semaphore_wait(in_sem.at[to], 1)

        block_copy(0, me, to, to).start()
        block_copy(1, me, to, to).start()

    half, hop = n // 2, n // 4
    facing = lax.rem(me + half, n)

    def to_relay(via, target):
        return pltpu.make_async_remote_copy(
            src_ref=v_in.at[:, pl.ds(pl.multiple_of(target * width, width), width)],
            dst_ref=relay_buf,
            send_sem=send_sem.at[3, target],
            recv_sem=relay_sem,
            device_id={"head": via},
            device_id_type=MESH,
        )

    def from_relay(source, target):
        return pltpu.make_async_remote_copy(
            src_ref=relay_buf,
            dst_ref=v_buf.at[pl.ds(pl.multiple_of(source * rows, rows), rows), :],
            send_sem=pass_sem,
            recv_sem=recv_sem.at[3, source],
            device_id={"head": target},
            device_id_type=MESH,
        )

    @pl.when(me < half)
    def _():
        to_relay(me + hop, facing).start()

    relays = jnp.logical_and(me >= hop, me < hop + half)
    for to in peers(n, me, near_first):
        block_copy(2, me, to, to).start()

    others = [lax.rem(me + d, n) for d in range(1, n)]

    def arrive(a):
        own[a].wait()
        for other in others:
            block_copy(a, other, other, other).wait_recv()

    g_copy.wait()
    arrive(0)
    arrive(1)

    @pl.when(relays)
    def _():
        to_relay(me + hop, me + hop).wait_recv()
        from_relay(me - hop, me + hop).start()

    for to in peers(n, me, ascending):

        @pl.when(jnp.logical_or(me >= half, to != facing))
        def _():
            block_copy(3, me, to, to).start()

    dk_acc[...] = jnp.zeros_like(dk_acc)
    dv_acc[...] = jnp.zeros_like(dv_acc)
    cross_rows = 256

    def cross_step(i, carry):
        at = pl.ds(pl.multiple_of(i * cross_rows, cross_rows), cross_rows)
        for h in range(groups):
            cols = pl.ds(h * HD, HD)
            q = q_buf[at, cols]
            g = g_buf[at, cols]
            kt = t_buf[:, pl.ds(2 * h * HD, HD)]
            vt = t_buf[:, pl.ds((2 * h + 1) * HD, HD)]
            x = dot(kt, q, 1, 1)
            e = jnp.exp2((x - jnp.max(x, axis=0, keepdims=True)) * factor)
            r = e * (1.0 / jnp.sum(e, axis=0, keepdims=True))
            rb = r.astype(BF16)
            dr = dot(vt, g, 1, 1)
            dx = (r * (dr - jnp.sum(dr * r, axis=0, keepdims=True))).astype(BF16)
            dk_acc[h] += dot(dx, q, 1, 0)
            dv_acc[h] += dot(rb, g, 1, 0)
            cross_buf[at, cols] = dot(rb, vt, 0, 0)
        return carry

    lax.fori_loop(0, length // cross_rows, cross_step, 0)
    for h in range(groups):
        tg_buf[:, pl.ds(2 * h * HD, HD)] = (dk_acc[h] * (HD ** -0.5)).astype(BF16)
        tg_buf[:, pl.ds((2 * h + 1) * HD, HD)] = dv_acc[h].astype(BF16)
    own_grad = pltpu.make_async_copy(
        tg_buf.at[pl.ds(pl.multiple_of(me * trows, trows), trows), :],
        tg_out.at[:, pl.ds(pl.multiple_of(me * twidth, twidth), twidth)],
        local_sem.at[5],
    )
    own_grad.start()
    def grad_copy(source, to, sem):
        return pltpu.make_async_remote_copy(
            src_ref=tg_buf.at[pl.ds(pl.multiple_of(to * trows, trows), trows), :],
            dst_ref=tg_out.at[:, pl.ds(pl.multiple_of(source * twidth, twidth), twidth)],
            send_sem=gsend_sem.at[sem],
            recv_sem=grecv_sem.at[source],
            device_id={"head": to},
            device_id_type=MESH,
        )

    for to in peers(n, me, ascending):

        grad_copy(me, to, to).start()

    arrive(2)
    block = 256

    def score_step(i, carry):
        at = pl.ds(pl.multiple_of(i * block, block), block)
        for h in range(groups):
            cols = pl.ds(h * HD, HD)
            s = dot(q_buf[at, cols], k_buf[:, cols], 1, 1)
            top = jnp.max(s, axis=1, keepdims=True)
            p_buf[h, at, :] = jnp.exp2((s - top) * factor).astype(BF16)
        return carry

    lax.fori_loop(0, length // block, score_step, 0)

    arrive(3)

    def out_copy(i):
        at = pl.ds(pl.multiple_of(i * block, block), block)
        return pltpu.make_async_copy(att_buf.at[at, :], att_out.at[at, :], out_sem.at[i])

    def value_step(i, carry):
        at = pl.ds(pl.multiple_of(i * block, block), block)
        for h in range(groups):
            cols = pl.ds(h * HD, HD)
            v = v_buf[:, cols]
            both = dot(p_buf[h, at, :], jnp.concatenate([v, jnp.ones_like(v)], axis=1), 1, 0)
            att_buf[at, cols] = (both[:, :HD] / both[:, HD:] + cross_buf[at, cols]).astype(BF16)
        out_copy(i).start()
        return carry

    lax.fori_loop(0, length // block, value_step, 0)

    own_grad.wait()

    @pl.when(relays)
    def _():
        from_relay(me - hop, me + hop).wait_send()

    for other in others:
        for a in range(4):
            block_copy(a, me, other, other).wait_send()
        grad_copy(me, other, other).wait_send()
        grad_copy(other, other, other).wait_recv()
    for i in range(length // block):
        out_copy(i).wait()


def place(a_in, b_in, a_out, b_out, sems):
    copies = []
    for src, dst, pieces in ((a_in, a_out, 4), (b_in, b_out, 2)):
        step = src.shape[0] // pieces
        for i in range(pieces):
            at = pl.ds(i * step, step)
            copies.append(pltpu.make_async_copy(src.at[at, :], dst.at[at, :], sems.at[len(copies)]))
    for copy in copies:
        copy.start()
    for copy in copies:
        copy.wait()


def per_device(n, queries, keys, values, text_kv, cotangent):
    rows, columns = queries.shape[1:]
    trows, tcolumns = text_kv.shape[1:]
    length, width = cotangent.shape[1:]
    twidth = tcolumns // n
    text = trows * n
    groups = width // HD
    attended, grad = pl.pallas_call(
        functools.partial(kernel, n),
        out_shape=(
            pltpu.VMEM((length, width), BF16),
            pltpu.VMEM((trows, tcolumns), BF16),
        ),
        in_specs=[pl.BlockSpec(memory_space=pl.ANY)] * 5,
        out_specs=(pl.BlockSpec(memory_space=pl.ANY),) * 2,
        scratch_shapes=[
            pltpu.VMEM((length, width), BF16),
            pltpu.VMEM((length, width), BF16),
            pltpu.VMEM((length, width), BF16),
            pltpu.VMEM((text, twidth), BF16),
            pltpu.VMEM((length, width), BF16),
            pltpu.VMEM((groups, length, length), BF16),
            pltpu.VMEM((length, width), F32),
            pltpu.VMEM((length, width), BF16),
            pltpu.VMEM((groups, text, HD), F32),
            pltpu.VMEM((groups, text, HD), F32),
            pltpu.VMEM((text, twidth), BF16),
            pltpu.VMEM((rows, width), BF16),
            pltpu.SemaphoreType.DMA((4, n)),
            pltpu.SemaphoreType.DMA((4, n)),
            pltpu.SemaphoreType.DMA((6,)),
            pltpu.SemaphoreType.DMA((length // 256,)),
            pltpu.SemaphoreType.DMA((n,)),
            pltpu.SemaphoreType.DMA((n,)),
            pltpu.SemaphoreType.REGULAR((n,)),
            pltpu.SemaphoreType.DMA,
            pltpu.SemaphoreType.DMA,
        ],
        compiler_params=pltpu.CompilerParams(
            collective_id=0, has_side_effects=True, vmem_limit_bytes=40 * 2**20
        ),
    )(*(pltpu.with_memory_space_constraint(x[0], pltpu.HBM) for x in (queries, keys, values, text_kv, cotangent)))
    attended, grad = pl.pallas_call(
        place,
        out_shape=(
            jax.ShapeDtypeStruct((length, width), BF16),
            jax.ShapeDtypeStruct((trows, tcolumns), BF16),
        ),
        in_specs=[pl.BlockSpec(memory_space=pl.ANY)] * 2,
        out_specs=(pl.BlockSpec(memory_space=pltpu.HBM),) * 2,
        scratch_shapes=[pltpu.SemaphoreType.DMA((6,))],
    )(*(pltpu.with_memory_space_constraint(x, pltpu.VMEM) for x in (attended, grad)))
    return attended[None], grad[None]


def solution(mesh):
    split = P(("seq", "rep"), "head", None)
    kept = P(("seq", "rep"), None, "head")
    return jax.shard_map(
        functools.partial(per_device, mesh.shape["head"]),
        mesh=mesh,
        in_specs=(split, split, split, split, kept),
        out_specs=(kept, split),
        check_vma=False,
    )
```

```python
import functools
import math

import jax
import jax.numpy as jnp
from jax import lax
from jax.experimental import pallas as pl
from jax.experimental.pallas import tpu as pltpu
from jax.sharding import PartitionSpec as P

HD = 128
MESH = pl.DeviceIdType.MESH
BF16 = jnp.bfloat16
F32 = jnp.float32


def dot(a, b, ca, cb):
    return lax.dot_general(a, b, (((ca,), (cb,)), ((), ())), preferred_element_type=F32)


def near_first(n, at):
    order = []
    for d in range(1, n // 2 + 1):
        order.append((at + d) % n)
        if n - d != d:
            order.append((at - d) % n)
    return order


def below_first(n, at):
    return [to for to in near_first(n, at) if to < at] + list(range(at + 1, n))


def ascending(n, at):
    return [to for to in range(n) if to != at]


def pick(me, column):
    value = jnp.int32(column[0])
    for at in range(1, len(column)):
        value = jnp.where(me == at, jnp.int32(column[at]), value)
    return value


def peers(n, me, order):
    table = [order(n, at) for at in range(n)]
    return [pick(me, [row[j] for row in table]) for j in range(n - 1)]


def kernel(
    n, q_in, k_in, v_in, t_in, g_in, att_out, tg_out,
    q_buf, k_buf, v_buf, t_buf, g_buf, p_buf, cross_buf, att_buf, dk_acc, dv_acc, tg_buf, relay_buf,
    send_sem, recv_sem, local_sem, out_sem, gsend_sem, grecv_sem, in_sem, relay_sem, pass_sem,
):
    me = lax.axis_index("head")
    rows = q_in.shape[0]
    trows = t_in.shape[0]
    width = q_buf.shape[1]
    twidth = t_buf.shape[1]
    length = q_buf.shape[0]
    groups = width // HD
    factor = HD ** -0.5 * math.log2(math.e)

    barrier = pltpu.get_barrier_semaphore()

    @pl.when(me > 0)
    def _():
        pl.semaphore_wait(barrier, 1)

    @pl.when(me < n - 1)
    def _():
        pl.semaphore_signal(barrier, inc=1, device_id={"head": lax.rem(me + 1, n)}, device_id_type=MESH)

    for w in range(n - 1):

        @pl.when(w < me)
        def _(w=w):
            pl.semaphore_signal(in_sem.at[me], inc=1, device_id={"head": w}, device_id_type=MESH)

    own = []
    for a, (src, dst, h, w) in enumerate(
        ((t_in, t_buf, trows, twidth), (q_in, q_buf, rows, width), (k_in, k_buf, rows, width), (v_in, v_buf, rows, width))
    ):
        copy = pltpu.make_async_copy(
            src.at[:, pl.ds(pl.multiple_of(me * w, w), w)],
            dst.at[pl.ds(pl.multiple_of(me * h, h), h), :],
            local_sem.at[a],
        )
        copy.start()
        own.append(copy)
    g_copy = pltpu.make_async_copy(g_in, g_buf, local_sem.at[4])
    g_copy.start()

    arrays = ((t_in, t_buf, trows, twidth), (q_in, q_buf, rows, width), (k_in, k_buf, rows, width), (v_in, v_buf, rows, width))

    def block_copy(a, source, to, sem):
        src, dst, h, w = arrays[a]
        return pltpu.make_async_remote_copy(
            src_ref=src.at[:, pl.ds(pl.multiple_of(to * w, w), w)],
            dst_ref=dst.at[pl.ds(pl.multiple_of(source * h, h), h), :],
            send_sem=send_sem.at[a, sem],
            recv_sem=recv_sem.at[a, source],
            device_id={"head": to},
            device_id_type=MESH,
        )

    for to in peers(n, me, below_first):

        @pl.when(to > me)
        def _():
            pl.semaphore_wait(in_sem.at[to], 1)

        block_copy(0, me, to, to).start()
        block_copy(1, me, to, to).start()

    half, hop = n // 2, n // 4
    facing = lax.rem(me + half, n)

    def to_relay(a, via, target):
        return pltpu.make_async_remote_copy(
            src_ref=arrays[a][0].at[:, pl.ds(pl.multiple_of(target * width, width), width)],
            dst_ref=relay_buf.at[a - 2],
            send_sem=send_sem.at[a, target],
            recv_sem=relay_sem.at[a - 2],
            device_id={"head": via},
            device_id_type=MESH,
        )

    def from_relay(a, source, target):
        return pltpu.make_async_remote_copy(
            src_ref=relay_buf.at[a - 2],
            dst_ref=arrays[a][1].at[pl.ds(pl.multiple_of(source * rows, rows), rows), :],
            send_sem=pass_sem.at[a - 2],
            recv_sem=recv_sem.at[a, source],
            device_id={"head": target},
            device_id_type=MESH,
        )

    @pl.when(me < half)
    def _():
        for a in (2, 3):
            to_relay(a, me + hop, facing).start()

    relays = jnp.logical_and(me >= hop, me < hop + half)
    for to in peers(n, me, near_first):

        @pl.when(jnp.logical_or(me >= half, to != facing))
        def _():
            block_copy(2, me, to, to).start()

    others = [lax.rem(me + d, n) for d in range(1, n)]

    def arrive(a):
        own[a].wait()
        for other in others:
            block_copy(a, other, other, other).wait_recv()

    g_copy.wait()
    arrive(0)
    arrive(1)

    @pl.when(relays)
    def _():
        for a in (2, 3):
            to_relay(a, me + hop, me + hop).wait_recv()
            from_relay(a, me - hop, me + hop).start()

    for to in peers(n, me, ascending):

        @pl.when(jnp.logical_or(me >= half, to != facing))
        def _():
            block_copy(3, me, to, to).start()

    dk_acc[...] = jnp.zeros_like(dk_acc)
    dv_acc[...] = jnp.zeros_like(dv_acc)
    cross_rows = 256

    def cross_step(i, carry):
        at = pl.ds(pl.multiple_of(i * cross_rows, cross_rows), cross_rows)
        for h in range(groups):
            cols = pl.ds(h * HD, HD)
            q = q_buf[at, cols]
            g = g_buf[at, cols]
            kt = t_buf[:, pl.ds(2 * h * HD, HD)]
            vt = t_buf[:, pl.ds((2 * h + 1) * HD, HD)]
            x = dot(kt, q, 1, 1)
            e = jnp.exp2((x - jnp.max(x, axis=0, keepdims=True)) * factor)
            r = e * (1.0 / jnp.sum(e, axis=0, keepdims=True))
            rb = r.astype(BF16)
            dr = dot(vt, g, 1, 1)
            dx = (r * (dr - jnp.sum(dr * r, axis=0, keepdims=True))).astype(BF16)
            dk_acc[h] += dot(dx, q, 1, 0)
            dv_acc[h] += dot(rb, g, 1, 0)
            cross_buf[at, cols] = dot(rb, vt, 0, 0)
        return carry

    lax.fori_loop(0, length // cross_rows, cross_step, 0)
    for h in range(groups):
        tg_buf[:, pl.ds(2 * h * HD, HD)] = (dk_acc[h] * (HD ** -0.5)).astype(BF16)
        tg_buf[:, pl.ds((2 * h + 1) * HD, HD)] = dv_acc[h].astype(BF16)
    own_grad = pltpu.make_async_copy(
        tg_buf.at[pl.ds(pl.multiple_of(me * trows, trows), trows), :],
        tg_out.at[:, pl.ds(pl.multiple_of(me * twidth, twidth), twidth)],
        local_sem.at[5],
    )
    own_grad.start()
    def grad_copy(source, to, sem):
        return pltpu.make_async_remote_copy(
            src_ref=tg_buf.at[pl.ds(pl.multiple_of(to * trows, trows), trows), :],
            dst_ref=tg_out.at[:, pl.ds(pl.multiple_of(source * twidth, twidth), twidth)],
            send_sem=gsend_sem.at[sem],
            recv_sem=grecv_sem.at[source],
            device_id={"head": to},
            device_id_type=MESH,
        )

    for to in peers(n, me, ascending):

        grad_copy(me, to, to).start()

    arrive(2)
    block = 256

    def score_step(i, carry):
        at = pl.ds(pl.multiple_of(i * block, block), block)
        for h in range(groups):
            cols = pl.ds(h * HD, HD)
            s = dot(q_buf[at, cols], k_buf[:, cols], 1, 1)
            top = jnp.max(s, axis=1, keepdims=True)
            p_buf[h, at, :] = jnp.exp2((s - top) * factor).astype(BF16)
        return carry

    lax.fori_loop(0, length // block, score_step, 0)

    arrive(3)

    def out_copy(i):
        at = pl.ds(pl.multiple_of(i * block, block), block)
        return pltpu.make_async_copy(att_buf.at[at, :], att_out.at[at, :], out_sem.at[i])

    def value_step(i, carry):
        at = pl.ds(pl.multiple_of(i * block, block), block)
        for h in range(groups):
            cols = pl.ds(h * HD, HD)
            v = v_buf[:, cols]
            both = dot(p_buf[h, at, :], jnp.concatenate([v, jnp.ones_like(v)], axis=1), 1, 0)
            att_buf[at, cols] = (both[:, :HD] / both[:, HD:] + cross_buf[at, cols]).astype(BF16)
        out_copy(i).start()
        return carry

    lax.fori_loop(0, length // block, value_step, 0)

    own_grad.wait()

    @pl.when(relays)
    def _():
        for a in (2, 3):
            from_relay(a, me - hop, me + hop).wait_send()

    for other in others:
        for a in range(4):
            block_copy(a, me, other, other).wait_send()
        grad_copy(me, other, other).wait_send()
        grad_copy(other, other, other).wait_recv()
    for i in range(length // block):
        out_copy(i).wait()


def place(a_in, b_in, a_out, b_out, sems):
    copies = []
    for src, dst, pieces in ((a_in, a_out, 4), (b_in, b_out, 2)):
        step = src.shape[0] // pieces
        for i in range(pieces):
            at = pl.ds(i * step, step)
            copies.append(pltpu.make_async_copy(src.at[at, :], dst.at[at, :], sems.at[len(copies)]))
    for copy in copies:
        copy.start()
    for copy in copies:
        copy.wait()


def per_device(n, queries, keys, values, text_kv, cotangent):
    rows, columns = queries.shape[1:]
    trows, tcolumns = text_kv.shape[1:]
    length, width = cotangent.shape[1:]
    twidth = tcolumns // n
    text = trows * n
    groups = width // HD
    attended, grad = pl.pallas_call(
        functools.partial(kernel, n),
        out_shape=(
            pltpu.VMEM((length, width), BF16),
            pltpu.VMEM((trows, tcolumns), BF16),
        ),
        in_specs=[pl.BlockSpec(memory_space=pl.ANY)] * 5,
        out_specs=(pl.BlockSpec(memory_space=pl.ANY),) * 2,
        scratch_shapes=[
            pltpu.VMEM((length, width), BF16),
            pltpu.VMEM((length, width), BF16),
            pltpu.VMEM((length, width), BF16),
            pltpu.VMEM((text, twidth), BF16),
            pltpu.VMEM((length, width), BF16),
            pltpu.VMEM((groups, length, length), BF16),
            pltpu.VMEM((length, width), F32),
            pltpu.VMEM((length, width), BF16),
            pltpu.VMEM((groups, text, HD), F32),
            pltpu.VMEM((groups, text, HD), F32),
            pltpu.VMEM((text, twidth), BF16),
            pltpu.VMEM((2, rows, width), BF16),
            pltpu.SemaphoreType.DMA((4, n)),
            pltpu.SemaphoreType.DMA((4, n)),
            pltpu.SemaphoreType.DMA((6,)),
            pltpu.SemaphoreType.DMA((length // 256,)),
            pltpu.SemaphoreType.DMA((n,)),
            pltpu.SemaphoreType.DMA((n,)),
            pltpu.SemaphoreType.REGULAR((n,)),
            pltpu.SemaphoreType.DMA((2,)),
            pltpu.SemaphoreType.DMA((2,)),
        ],
        compiler_params=pltpu.CompilerParams(
            collective_id=0, has_side_effects=True, vmem_limit_bytes=40 * 2**20
        ),
    )(*(pltpu.with_memory_space_constraint(x[0], pltpu.HBM) for x in (queries, keys, values, text_kv, cotangent)))
    attended, grad = pl.pallas_call(
        place,
        out_shape=(
            jax.ShapeDtypeStruct((length, width), BF16),
            jax.ShapeDtypeStruct((trows, tcolumns), BF16),
        ),
        in_specs=[pl.BlockSpec(memory_space=pl.ANY)] * 2,
        out_specs=(pl.BlockSpec(memory_space=pltpu.HBM),) * 2,
        scratch_shapes=[pltpu.SemaphoreType.DMA((6,))],
    )(*(pltpu.with_memory_space_constraint(x, pltpu.VMEM) for x in (attended, grad)))
    return attended[None], grad[None]


def solution(mesh):
    split = P(("seq", "rep"), "head", None)
    kept = P(("seq", "rep"), None, "head")
    return jax.shard_map(
        functools.partial(per_device, mesh.shape["head"]),
        mesh=mesh,
        in_specs=(split, split, split, split, kept),
        out_specs=(kept, split),
        check_vma=False,
    )
```
